256 devices in a mesh: depth: 16 (over x, y), tile: 16 (over z, core).
Axes of the slice: x: 4, y: 4, z: 8, core: 2. Of those that a mesh axis runs over, the one named last changes fastest.
Arguments:
- pool: bfloat16 [16, 768, 4, 4, 4096], P('depth', 'tile'), may hold values from 0 to 1
- page_table: int32 [16, 512], P('depth'), may hold values from -1 to 767, as said below
- tf_bins: int32 [256], replicated, may hold values from 0 to 15
- palette: float32 [4, 16], replicated, may hold values from 0.05 to 1
Outputs:
- image: float32 [4, 512, 4096], P(None, 'tile', 'depth')
The draws below stay inside these ranges and needn't reach their ends.
Inputs may be any that keep to these rules, and one draw needn't show every extreme that they name: `page_table`: row d gives, for each footprint f of slab d, the pool page (pages numbered over the devices of the tile axis in order, 48 to a device) that holds its brick, or -1 for a culled brick; the nonnegative values of a row are distinct; footprint f belongs to image tile f // 32; in a row, at most 2 footprints of one image tile have their pages on one device, and exactly 2 for some pairs of tile and device.
All inputs are finite; a program needn't handle non-finite values.
Results may differ from the reference program's by a relative error of at most 0.0003.
Values may be sent and summed in bfloat16 or wider, within the bound.
No kernel may reach another device: no remote copies, remote signals or barrier semaphores. Data moves between devices by JAX's collectives and lax.ppermute only.
A program may use at most 128 MiB of HBM per device.

```python
import jax
import jax.numpy as jnp
from jax import lax

FPIX = 4096
BD = 4
CAP = 2
NB = 256
PAL = 16
FOOT = 32
PAGES = 48
NFOOT = 512
POOL = 768
N_DEPTH = 16
N_TILE = 16


def draw_page_table(key, part):
    key = jax.random.fold_in(key, 7)
    shift_key, order_key, cull_key = jax.random.split(key, 3)
    groups = FOOT // CAP
    shift_keys = jax.random.split(shift_key, N_DEPTH)
    offsets = jax.vmap(lambda single: jax.random.permutation(single, N_TILE)[:groups])(shift_keys)
    order_keys = jax.random.split(order_key, N_DEPTH * N_TILE)
    shuffled = jax.vmap(lambda single: jax.random.permutation(single, PAGES - 1))(order_keys)
    orders = jnp.concatenate([jnp.full((N_DEPTH * N_TILE, 1), PAGES - 1, jnp.int32), shuffled.astype(jnp.int32)], axis=1)
    orders = orders.reshape(N_DEPTH, N_TILE, PAGES)
    footprint = jnp.arange(FOOT * N_TILE)
    owner_index = footprint // FOOT
    within = footprint % FOOT
    group_index = within // CAP
    holder = (owner_index[None, :] + offsets[:, group_index]) % N_TILE
    depth_index = jnp.arange(N_DEPTH)[:, None]
    local_page = orders[depth_index, holder, within[None, :]]
    page_index = holder * PAGES + local_page
    chance = jax.random.randint(cull_key, (N_DEPTH, FOOT * N_TILE), 0, 8)
    forced = footprint == FOOT * N_TILE - 1
    culled = (group_index[None, :] > 0) & ((chance < owner_index[None, :] % 4) | forced[None, :])
    return jnp.where(culled, -1, page_index).astype(jnp.int32)


def set_ends(array, key, low, largest):
    place = [jax.random.randint(jax.random.fold_in(key, axis), (), 0, length) for axis, length in enumerate(array.shape)]
    longest = array.shape.index(max(array.shape))
    next_to = place[:longest] + [(place[longest] + 1) % array.shape[longest]] + place[longest + 1:]
    return array.at[tuple(place)].set(low).at[tuple(next_to)].set(largest)


def steps_of(stream_key, dims, cuts, least, high):
    loudness, own = 1.0, jax.random.fold_in(stream_key, 6)
    for dim, shards_of in cuts:
        steps = jnp.exp(jax.random.uniform(jax.random.fold_in(own, dim), (shards_of,), jnp.float32, least / len(cuts), high / len(cuts)))
        loudness = loudness * jnp.repeat(steps, dims[dim] // shards_of).reshape([-1 if axis == dim else 1 for axis in range(len(dims))])
    return loudness


def setup_inputs(seed: int = 0) -> dict:
    splits = jax.random.split(jax.random.key(seed), 5)
    pool = jnp.clip(1.0 * jax.random.uniform(splits[0], (N_DEPTH, POOL, 4, BD, FPIX), jnp.float32) ** steps_of(splits[0], (N_DEPTH, POOL, 4, BD, FPIX), ((0, 16), (1, 16)), -0.2, 0.2), 0.0, 1.0).astype(jnp.bfloat16)
    page_table = draw_page_table(jax.random.fold_in(splits[4], 71), 0)
    tf_bins = set_ends(jax.random.randint(splits[2], (NB,), 0, PAL), jax.random.fold_in(splits[2], 1), 0, PAL - 1).astype(jnp.int32)
    palette = jnp.clip(jax.random.uniform(splits[3], (4, PAL), jnp.float32, 0.05, 1.0), 0.05, 1.0)
    return {"pool": pool, "page_table": page_table, "tf_bins": tf_bins, "palette": palette}


LIGHT_X = 0.48
LIGHT_Y = 0.6
LIGHT_Z = 0.64


def render_pages(bricks, colour_table):
    values = bricks.astype(jnp.float32)
    scaled = values[:, 0] * (NB - 1)
    lower_bin = jnp.clip(jnp.floor(scaled), 0, NB - 2)
    weight_up = scaled - lower_bin
    lower_index = lower_bin.astype(jnp.int32)
    lower_value = jnp.take(colour_table, lower_index, axis=1)
    upper_value = jnp.take(colour_table, lower_index + 1, axis=1)
    rgba = lower_value * (1.0 - weight_up) + upper_value * weight_up
    normal = values[:, 1:4] * 2.0 - 1.0
    facing = LIGHT_X * normal[:, 0] + LIGHT_Y * normal[:, 1] + LIGHT_Z * normal[:, 2]
    shading = 0.5 + 0.5 * jnp.tanh(facing)
    optical = rgba[3] * (4.0 / (BD * N_DEPTH))
    through = jnp.cumsum(optical, axis=1)
    weights = jnp.exp(optical - through) - jnp.exp(-through)
    colour = jnp.sum(rgba[0:3] * shading[None] * weights[None], axis=2)
    remaining = jnp.exp(-through[:, -1])
    return jnp.concatenate([colour, remaining[None]], axis=0)


def reference(pool, page_table, tf_bins, palette):
    colour_table = jnp.take(palette, tf_bins, axis=1)
    clear = jnp.concatenate([jnp.zeros((3,), jnp.float32), jnp.ones((1,), jnp.float32)])[:, None, None]

    def one_row(inputs):
        row_pool, row_table = inputs
        gathered = row_pool[jnp.maximum(row_table, 0)]
        images = render_pages(gathered, colour_table)
        return jnp.where(row_table[None, :, None] >= 0, images, clear)

    slabs = lax.map(one_row, (pool, page_table))

    def compose(carry, layer):
        merged = jnp.concatenate([carry[0:3] + carry[3:4] * layer[0:3], carry[3:4] * layer[3:4]], axis=0)
        return merged, None

    initial = jnp.concatenate([jnp.zeros((3, NFOOT, FPIX), jnp.float32), jnp.ones((1, NFOOT, FPIX), jnp.float32)], axis=0)
    image, _ = lax.scan(compose, initial, slabs)
    return image
```

```python
import functools

import jax
import jax.numpy as jnp
from jax import lax
from jax.experimental import pallas as pl
from jax.experimental.pallas import tpu as pltpu
from jax.sharding import PartitionSpec as P

BINS = 256
LANES = 128
SUB = 8
CAP = 2
LIGHT_X = 0.48
LIGHT_Y = 0.6
LIGHT_Z = 0.64
LOG2E = 1.4426950408889634
FULL = 65535.0
REACH = 0.2213
AHEAD = 2
SLOTS = 4


def render_kernel(table_ref, bins_ref, palette_ref, pool_ref, out_ref, pages, cells32, wide, sems, *, tiles, per_tile, page_count):
    mine = lax.axis_index("tile")
    first_page = mine * page_count

    def find(tile):
        one = jnp.int32(-1)
        two = jnp.int32(-1)
        for foot in range(per_tile):
            local = table_ref[0, tile * per_tile + foot] - first_page
            here = (local >= 0) & (local < page_count)
            two = jnp.where(here & (one >= 0), local, two)
            one = jnp.where(here & (one < 0), local, one)
        return jnp.maximum(one, 0), jnp.maximum(two, 0)

    def fetch(slot, rank, page):
        return pltpu.make_async_copy(pool_ref.at[page], pages.at[slot, rank], sems.at[slot, rank])

    def begin(tile):
        picked = find(tile)
        for rank in range(CAP):
            fetch(lax.rem(tile, SLOTS), rank, picked[rank]).start()

    for tile in range(AHEAD):
        begin(jnp.int32(tile))

    def gather(table, index):
        return jnp.take_along_axis(table, index, axis=1, mode="promise_in_bounds")

    wide[...] = jnp.zeros_like(wide)
    wide[0:4, 0:16] = palette_ref[...]
    palette = wide[...]
    low_bins = jnp.broadcast_to(bins_ref[0:1, :], (SUB, LANES))
    high_bins = jnp.broadcast_to(bins_ref[1:2, :], (SUB, LANES))
    lane = lax.broadcasted_iota(jnp.int32, (SUB, LANES), 1)
    zero = jnp.zeros((SUB, LANES), jnp.int32)
    following = (lane + 1) & (LANES - 1)
    high_next = gather(high_bins, following)
    low_next = jnp.where(lane == LANES - 1, gather(high_bins, zero), gather(low_bins, following))

    def coded(bins):
        return (gather(palette, bins) * FULL + 0.5).astype(jnp.int32)

    low_table = coded(low_bins) | lax.shift_left(coded(low_next), 16)
    high_table = coded(high_bins) | lax.shift_left(coded(high_next), 16)
    tables = []
    for channel in range(4):
        tables.append(
            tuple(jnp.broadcast_to(t[channel : channel + 1, :], (SUB, LANES)) for t in (low_table, high_table))
        )

    def one_tile(tile, _):
        @pl.when(tile + AHEAD < tiles)
        def _():
            begin(tile + AHEAD)

        slot = lax.rem(tile, SLOTS)
        for rank in range(CAP):
            fetch(slot, rank, 0).wait()
            for field in range(4):
                cells32[rank, field] = pages[slot, rank, field].astype(jnp.float32)
            for half in range(2):
                for odd in range(2):
                    colour = [None] * 3
                    through = None
                    before = None
                    for cell in range(4):
                        rows = pl.ds(64 * half + 4 * odd + cell, SUB, stride=8)
                        scalar, normal_x, normal_y, normal_z = (cells32[rank, field, rows, :] for field in range(4))
                        scaled = scalar * (BINS - 1.0)
                        index = jnp.minimum(scaled.astype(jnp.int32), BINS - 2)
                        up = scaled - index.astype(jnp.float32)
                        upper_half = index >= LANES
                        lane_index = index & (LANES - 1)
                        rgba = []
                        for low, high in tables:
                            both = jnp.where(upper_half, gather(high, lane_index), gather(low, lane_index))
                            here = (both & 0xFFFF).astype(jnp.float32)
                            beyond = lax.shift_right_logical(both, 16).astype(jnp.float32)
                            rgba.append(here + (beyond - here) * up)
                        facing = (
                            normal_x * (2 * LIGHT_X)
                            + normal_y * (2 * LIGHT_Y)
                            + normal_z * (2 * LIGHT_Z)
                            - (LIGHT_X + LIGHT_Y + LIGHT_Z)
                        )
                        shading = 0.5 + 0.5 * jnp.tanh(facing)
                        optical = rgba[3] * (-LOG2E / (16.0 * FULL))
                        through = optical if cell == 0 else through + optical
                        after = jnp.exp2(through)
                        weight = shading * ((1.0 if cell == 0 else before) - after)
                        before = after
                        for c in range(3):
                            term = rgba[c] * weight
                            colour[c] = term if cell == 0 else colour[c] + term
                    coded_parts = []
                    for c in range(3):
                        square = colour[c] * (FULL / REACH)
                        root = square * lax.rsqrt(jnp.maximum(square, 1e-20))
                        coded_parts.append((root + 0.5).astype(jnp.int32))
                    coded_parts.append(((1.0 - before) * (FULL / REACH) + 0.5).astype(jnp.int32))
                    row = rank * 4 + odd
                    place = pl.ds(SUB * half, SUB)
                    out_ref[place, tile, row, :] = coded_parts[0] | lax.shift_left(coded_parts[1], 16)
                    out_ref[place, tile, row + 2, :] = coded_parts[2] | lax.shift_left(coded_parts[3], 16)
        return 0

    lax.fori_loop(0, tiles, one_tile, 0)


def compose_kernel(source_ref, received_ref, out_ref, ordered, *, depths, per_tile):
    groups = per_tile // SUB

    def one_depth(depth, state):
        for foot in range(per_tile):
            source = source_ref[depth, foot]
            block = received_ref[pl.ds(pl.multiple_of(jnp.maximum(source, 0) * 4, 4), 4), :]
            ordered[depth, 4 * foot : 4 * foot + 4, :] = jnp.where(source >= 0, block, 0)
        new = []
        for group in range(groups):
            for odd in range(2):
                red, green, blue, clear = state[group * 2 + odd]
                first = ordered[depth, pl.ds(32 * group + odd, SUB, stride=4), :]
                second = ordered[depth, pl.ds(32 * group + 2 + odd, SUB, stride=4), :]

                def squared(x):
                    x = x.astype(jnp.float32)
                    return x * x

                scaled = clear * (REACH / (FULL * FULL))
                red = red + scaled * squared(first & 0xFFFF)
                green = green + scaled * squared(lax.shift_right_logical(first, 16))
                blue = blue + scaled * squared(second & 0xFFFF)
                clear = clear - clear * (lax.shift_right_logical(second, 16).astype(jnp.float32) * (REACH / FULL))
                new.append((red, green, blue, clear))
        return new

    none = jnp.zeros((SUB, LANES), jnp.float32)
    state = [(none, none, none, none + 1.0) for _ in range(groups * 2)]
    state = lax.fori_loop(0, depths, one_depth, state)
    for group in range(groups):
        for odd in range(2):
            for c in range(4):
                out_ref[c, SUB * group : SUB * group + SUB, LANES * odd : LANES * odd + LANES] = state[group * 2 + odd][c]


def per_device(pool, page_table, tf_bins, palette):
    tiles = lax.axis_size("tile")
    depths = lax.axis_size("depth")
    tile = lax.axis_index("tile")
    page_count, cells, pixels = pool.shape[1], pool.shape[3], pool.shape[4]
    per_tile = page_table.shape[1] // tiles
    columns = pixels // LANES

    rows = page_table[:, :]
    gathered = lax.all_gather(rows, "depth", axis=0, tiled=True)

    bricks = pool[0].reshape(page_count, 4, cells, columns, LANES).transpose(0, 1, 3, 2, 4)
    bricks = bricks.reshape(page_count, 4, columns * cells, LANES)
    messages = pl.pallas_call(
        functools.partial(render_kernel, tiles=tiles, per_tile=per_tile, page_count=page_count),
        out_shape=jax.ShapeDtypeStruct((depths, tiles, SUB, LANES), jnp.int32),
        in_specs=[
            pl.BlockSpec(memory_space=pltpu.SMEM),
            pl.BlockSpec(memory_space=pltpu.VMEM),
            pl.BlockSpec(memory_space=pltpu.VMEM),
            pl.BlockSpec(memory_space=pltpu.HBM),
        ],
        out_specs=pl.BlockSpec(memory_space=pltpu.VMEM),
        scratch_shapes=[
            pltpu.VMEM((SLOTS, CAP, 4, columns * cells, LANES), jnp.bfloat16),
            pltpu.VMEM((CAP, 4, columns * cells, LANES), jnp.float32),
            pltpu.VMEM((SUB, LANES), jnp.float32),
            pltpu.SemaphoreType.DMA((SLOTS, CAP)),
        ],
        compiler_params=pltpu.CompilerParams(vmem_limit_bytes=60 * 1024 * 1024),
        name="render",
    )(page_table, tf_bins.reshape(2, LANES), palette, bricks)

    received = lax.all_to_all(
        messages.reshape(depths * tiles, SUB, LANES), ("depth", "tile"), split_axis=0, concat_axis=0, tiled=True
    )

    own = lax.dynamic_slice_in_dim(gathered, tile * per_tile, per_tile, 1)
    holder = jnp.where(own >= 0, own // page_count, -1)
    foot = jnp.arange(per_tile)
    earlier = (holder[:, :, None] == holder[:, None, :]) & (foot[None, :, None] > foot[None, None, :])
    rank = jnp.any(earlier, axis=2).astype(jnp.int32)
    source = (jnp.arange(depths)[:, None] * tiles + holder) * CAP + rank
    source = jnp.where(own >= 0, source, -1)

    return pl.pallas_call(
        functools.partial(compose_kernel, depths=depths, per_tile=per_tile),
        out_shape=jax.ShapeDtypeStruct((4, per_tile, pixels // depths), jnp.float32),
        in_specs=[pl.BlockSpec(memory_space=pltpu.SMEM), pl.BlockSpec(memory_space=pltpu.VMEM)],
        out_specs=pl.BlockSpec(memory_space=pltpu.VMEM),
        scratch_shapes=[pltpu.VMEM((depths, 4 * per_tile, LANES), jnp.int32)],
        compiler_params=pltpu.CompilerParams(vmem_limit_bytes=24 * 1024 * 1024),
        name="compose",
    )(source, received.reshape(depths * tiles * SUB, LANES))


def solution(mesh):
    in_specs = (P("depth", "tile", None, None, None), P("depth", None), P(), P())
    out_specs = P(None, "tile", "depth")
    return jax.shard_map(per_device, mesh=mesh, in_specs=in_specs, out_specs=out_specs, check_vma=False)
```

```python
import functools

import jax
import jax.numpy as jnp
from jax import lax
from jax.experimental import pallas as pl
from jax.experimental.pallas import tpu as pltpu
from jax.sharding import PartitionSpec as P

BINS = 256
LANES = 128
SUB = 8
CAP = 2
FOOT = 32
SHARE = 256
LIGHT_X = 0.48
LIGHT_Y = 0.6
LIGHT_Z = 0.64
LOG2E = 1.4426950408889634
FULL = 65535.0
HALF = 32768
REACH = 0.2213
KEY = 64
SHIFT = 16
STEP = 4


def render_kernel(
    table_ref, bins_ref, palette_ref, pool_ref, out_ref, pages, cells32, wide, staged, found_scalar, sems, out_sems, *, tiles, page_count
):
    local = table_ref[...] - lax.axis_index("tile") * page_count
    here = (local >= 0) & (local < page_count)
    key = (lax.broadcasted_iota(jnp.int32, local.shape, 1) & (FOOT - 1)) * KEY + local
    least = jnp.where(here, key, FOOT * KEY)
    largest = jnp.where(here, key, -1)
    step = 1
    while step < FOOT:
        least = jnp.minimum(least, pltpu.roll(least, step, 1))
        largest = jnp.maximum(largest, pltpu.roll(largest, step, 1))
        step *= 2
    one = jnp.where(largest >= 0, KEY | (least & (KEY - 1)), 0)
    two = jnp.where(largest > least, KEY | (largest & (KEY - 1)), 0)
    both_found = one | lax.shift_left(two, SHIFT)
    picked = [both_found[tile // 4, (tile % 4) * FOOT + FOOT - 1] for tile in range(tiles)]

    def fetch(tile, rank, page):
        return pltpu.make_async_copy(pool_ref.at[page], pages.at[tile, rank], sems.at[tile, rank])

    def begin(tile):
        both = picked[tile]
        found_scalar[tile] = both
        fetch(tile, 0, both & (KEY - 1)).start()
        fetch(tile, 1, lax.shift_right_logical(both, SHIFT) & (KEY - 1)).start()

    for tile in range(tiles):
        begin(tile)

    def gather(table, index):
        return jnp.take_along_axis(table, index, axis=1, mode="promise_in_bounds")

    wide[...] = jnp.zeros_like(wide)
    wide[0:4, 0:16] = palette_ref[...]
    palette = wide[...]
    low_bins = jnp.broadcast_to(bins_ref[0:1, :], (SUB, LANES))
    high_bins = jnp.broadcast_to(bins_ref[1:2, :], (SUB, LANES))
    lane = lax.broadcasted_iota(jnp.int32, (SUB, LANES), 1)
    zero = jnp.zeros((SUB, LANES), jnp.int32)
    following = (lane + 1) & (LANES - 1)
    high_next = gather(high_bins, following)
    low_next = jnp.where(lane == LANES - 1, gather(high_bins, zero), gather(low_bins, following))

    def coded(bins, next_bins):
        value = gather(palette, bins) * FULL
        whole = (value + 0.5).astype(jnp.int32)
        change = (gather(palette, next_bins) * FULL - value) * 0.5 - whole.astype(jnp.float32) * (1.0 / 65536.0)
        step = (change + (HALF + 0.5)).astype(jnp.int32) - HALF
        return lax.shift_left(step, 16) | whole

    low_table = coded(low_bins, low_next)
    high_table = coded(high_bins, high_next)
    tables = []
    for channel in range(4):
        tables.append(
            tuple(jnp.broadcast_to(t[channel : channel + 1, :], (SUB, LANES)) for t in (low_table, high_table))
        )

    def send(turn):
        return pltpu.make_async_copy(staged.at[turn], out_ref.at[:, pl.ds(turn * STEP, STEP)], out_sems.at[turn])

    def some_tiles(turn, _):
        first = turn * STEP
        for part in range(CAP * STEP):
            fetch(first + part // CAP, part % CAP, 0).wait()
        for part in range(CAP * STEP):
            tile, rank = first + part // CAP, part % CAP
            filled = (found_scalar[tile] & (KEY << (SHIFT * rank))) != 0
            for field in range(4):
                cells32[part, field] = pages[tile, rank, field].astype(jnp.float32)
            for half in range(2):
                for odd in range(2):
                    colour = [None] * 3
                    through = None
                    before = None
                    for cell in range(4):
                        rows = pl.ds(64 * half + 4 * odd + cell, SUB, stride=8)
                        scalar, normal_x, normal_y, normal_z = (cells32[part, field, rows, :] for field in range(4))
                        scaled = scalar * (BINS - 1.0)
                        index = scaled.astype(jnp.int32)
                        up = (scaled - index.astype(jnp.float32)) * (1.0 / HALF)
                        upper_half = index >= LANES
                        lane_index = index & (LANES - 1)
                        rgba = []
                        for low, high in tables:
                            both = jnp.where(upper_half, gather(high, lane_index), gather(low, lane_index))
                            rgba.append((both & 0xFFFF).astype(jnp.float32) + both.astype(jnp.float32) * up)
                        facing = (
                            normal_x * (2 * LIGHT_X)
                            + normal_y * (2 * LIGHT_Y)
                            + normal_z * (2 * LIGHT_Z)
                            - (LIGHT_X + LIGHT_Y + LIGHT_Z)
                        )
                        shading = 1.0 + jnp.tanh(facing)
                        optical = rgba[3] * (-LOG2E / (16.0 * FULL))
                        through = optical if cell == 0 else through + optical
                        after = jnp.exp2(through)
                        weight = shading * ((1.0 if cell == 0 else before) - after)
                        before = after
                        for c in range(3):
                            term = rgba[c] * weight
                            colour[c] = term if cell == 0 else colour[c] + term
                    coded_parts = []
                    for c in range(3):
                        square = colour[c] * (0.5 * FULL / REACH)
                        root = square * lax.rsqrt(jnp.maximum(square, 1e-20))
                        coded_parts.append((root + 0.5).astype(jnp.int32))
                    coded_parts.append(((1.0 - before) * (FULL / REACH) + 0.5).astype(jnp.int32))
                    row = rank * 4 + odd
                    words = (
                        coded_parts[0] | lax.shift_left(coded_parts[1], 16),
                        coded_parts[2] | lax.shift_left(coded_parts[3], 16),
                    )
                    place = pl.ds(SUB * half, SUB)
                    for word in range(2):
                        staged[turn, place, part // CAP, row + 2 * word, :] = jnp.where(filled, words[word], 0)
        send(turn).start()
        return 0

    lax.fori_loop(0, tiles // STEP, some_tiles, 0)
    for turn in range(tiles // STEP):
        send(turn).wait()


def compose_kernel(source_ref, received_ref, out_ref, ordered, *, depths, per_tile):
    groups = per_tile // SUB

    def one_depth(depth, state):
        for foot in range(per_tile):
            source = pl.multiple_of(source_ref[depth, foot], 4)
            ordered[depth, 4 * foot : 4 * foot + 4, :] = received_ref[pl.ds(source, 4), :]
        new = []
        for group in range(groups):
            for odd in range(2):
                red, green, blue, clear = state[group * 2 + odd]
                first = ordered[depth, pl.ds(32 * group + odd, SUB, stride=4), :]
                second = ordered[depth, pl.ds(32 * group + 2 + odd, SUB, stride=4), :]

                def squared(x):
                    x = x.astype(jnp.float32)
                    return x * x

                scaled = clear * (REACH / (FULL * FULL))
                red = red + scaled * squared(first & 0xFFFF)
                green = green + scaled * squared(lax.shift_right_logical(first, 16))
                blue = blue + scaled * squared(second & 0xFFFF)
                clear = clear - clear * (lax.shift_right_logical(second, 16).astype(jnp.float32) * (REACH / FULL))
                new.append((red, green, blue, clear))
        return new

    none = jnp.zeros((SUB, LANES), jnp.float32)
    state = [(none, none, none, none + 1.0) for _ in range(groups * 2)]
    state = lax.fori_loop(0, depths, one_depth, state, unroll=4)
    for group in range(groups):
        for odd in range(2):
            for c in range(4):
                out_ref[c, SUB * group : SUB * group + SUB, LANES * odd : LANES * odd + LANES] = state[group * 2 + odd][c]


def render_messages(page_table, tf_bins, palette, pool):
    page_count, cells, pixels = pool.shape[1], pool.shape[3], pool.shape[4]
    depths, tiles = pixels // SHARE, page_table.shape[1] // FOOT
    columns = pixels // LANES
    bricks = pool[0].reshape(page_count, 4, cells, columns, LANES).transpose(0, 1, 3, 2, 4)
    bricks = bricks.reshape(page_count, 4, columns * cells, LANES)
    return pl.pallas_call(
        functools.partial(render_kernel, tiles=tiles, page_count=page_count),
        out_shape=jax.ShapeDtypeStruct((depths, tiles, SUB, LANES), jnp.int32),
        in_specs=[
            pl.BlockSpec(memory_space=pltpu.VMEM),
            pl.BlockSpec(memory_space=pltpu.VMEM),
            pl.BlockSpec(memory_space=pltpu.VMEM),
            pl.BlockSpec(memory_space=pltpu.HBM),
        ],
        out_specs=pl.BlockSpec(memory_space=pltpu.HBM),
        scratch_shapes=[
            pltpu.VMEM((tiles, CAP, 4, columns * cells, LANES), jnp.bfloat16),
            pltpu.VMEM((CAP * STEP, 4, columns * cells, LANES), jnp.float32),
            pltpu.VMEM((SUB, LANES), jnp.float32),
            pltpu.VMEM((tiles // STEP, depths, STEP, SUB, LANES), jnp.int32),
            pltpu.SMEM((tiles,), jnp.int32),
            pltpu.SemaphoreType.DMA((tiles, CAP)),
            pltpu.SemaphoreType.DMA((tiles // STEP,)),
        ],
        compiler_params=pltpu.CompilerParams(vmem_limit_bytes=60 * 1024 * 1024),
        name="render",
    )(page_table.reshape(FOOT * tiles // LANES, LANES), tf_bins.reshape(2, LANES), palette, bricks)


def per_device(pool, page_table, tf_bins, palette):
    tiles = lax.axis_size("tile")
    depths = lax.axis_size("depth")
    tile = lax.axis_index("tile")
    page_count, cells, pixels = pool.shape[1], pool.shape[3], pool.shape[4]
    per_tile = page_table.shape[1] // tiles

    rows = page_table[:, :]
    gathered = lax.all_gather(rows, "depth", axis=0, tiled=True)

    messages = render_messages(page_table, tf_bins, palette, pool)
    received = lax.all_to_all(
        messages.reshape(depths * tiles, SUB, LANES), ("depth", "tile"), split_axis=0, concat_axis=0, tiled=True
    )

    own = lax.dynamic_slice_in_dim(gathered, tile * per_tile, per_tile, 1)
    holder = jnp.where(own >= 0, own // page_count, -1)
    foot = jnp.arange(per_tile)
    earlier = (holder[:, :, None] == holder[:, None, :]) & (foot[None, :, None] > foot[None, None, :])
    rank = jnp.any(earlier, axis=2).astype(jnp.int32)
    source = (jnp.arange(depths)[:, None] * tiles + holder) * CAP + rank
    held = jnp.sum((holder[:, None, :] == jnp.arange(tiles)[None, :, None]).astype(jnp.int32), axis=2)
    last = (jnp.arange(depths)[:, None] * tiles + jnp.arange(tiles)[None, :]) * CAP + CAP - 1
    empty = jnp.max(jnp.where(held < CAP, last, 0), axis=1)
    source = jnp.where(own >= 0, source, empty[:, None]) * 4

    return pl.pallas_call(
        functools.partial(compose_kernel, depths=depths, per_tile=per_tile),
        out_shape=jax.ShapeDtypeStruct((4, per_tile, pixels // depths), jnp.float32),
        in_specs=[pl.BlockSpec(memory_space=pltpu.SMEM), pl.BlockSpec(memory_space=pltpu.VMEM)],
        out_specs=pl.BlockSpec(memory_space=pltpu.VMEM),
        scratch_shapes=[pltpu.VMEM((depths, 4 * per_tile, LANES), jnp.int32)],
        compiler_params=pltpu.CompilerParams(vmem_limit_bytes=24 * 1024 * 1024),
        name="compose",
    )(source, received.reshape(depths * tiles * SUB, LANES))


def solution(mesh):
    in_specs = (P("depth", "tile", None, None, None), P("depth", None), P(), P())
    out_specs = P(None, "tile", "depth")
    return jax.shard_map(per_device, mesh=mesh, in_specs=in_specs, out_specs=out_specs, check_vma=False)
```

```python
import functools

import jax
import jax.numpy as jnp
from jax import lax
from jax.experimental import pallas as pl
from jax.experimental.pallas import tpu as pltpu
from jax.sharding import PartitionSpec as P

BINS = 256
LANES = 128
SUB = 8
CAP = 2
FOOT = 32
SHARE = 256
LIGHT_X = 0.48
LIGHT_Y = 0.6
LIGHT_Z = 0.64
LOG2E = 1.4426950408889634
FULL = 65535.0
HALF = 32768
REACH = 0.2213
KEY = 64
SHIFT = 16
STEP = 4


def render_kernel(
    table_ref, bins_ref, palette_ref, pool_ref, out_ref, pages, cells32, wide, staged, found_scalar, sems, out_sems, *, tiles, page_count
):
    local = table_ref[...] - lax.axis_index("tile") * page_count
    here = (local >= 0) & (local < page_count)
    key = (lax.broadcasted_iota(jnp.int32, local.shape, 1) & (FOOT - 1)) * KEY + local
    least = jnp.where(here, key, FOOT * KEY)
    largest = jnp.where(here, key, -1)
    step = 1
    while step < FOOT:
        least = jnp.minimum(least, pltpu.roll(least, step, 1))
        largest = jnp.maximum(largest, pltpu.roll(largest, step, 1))
        step *= 2
    one = jnp.where(largest >= 0, KEY | (least & (KEY - 1)), 0)
    two = jnp.where(largest > least, KEY | (largest & (KEY - 1)), 0)
    both_found = one | lax.shift_left(two, SHIFT)
    picked = [both_found[tile // 4, (tile % 4) * FOOT + FOOT - 1] for tile in range(tiles)]

    def fetch(tile, rank, page):
        return pltpu.make_async_copy(pool_ref.at[page], pages.at[tile, rank], sems.at[tile, rank])

    def begin(tile):
        both = picked[tile]
        found_scalar[tile] = both
        fetch(tile, 0, both & (KEY - 1)).start()
        fetch(tile, 1, lax.shift_right_logical(both, SHIFT) & (KEY - 1)).start()

    for tile in range(tiles):
        begin(tile)

    def gather(table, index):
        return jnp.take_along_axis(table, index, axis=1, mode="promise_in_bounds")

    wide[...] = jnp.zeros_like(wide)
    wide[0:4, 0:16] = palette_ref[...]
    palette = wide[...]
    low_bins = jnp.broadcast_to(bins_ref[0:1, :], (SUB, LANES))
    high_bins = jnp.broadcast_to(bins_ref[1:2, :], (SUB, LANES))
    lane = lax.broadcasted_iota(jnp.int32, (SUB, LANES), 1)
    zero = jnp.zeros((SUB, LANES), jnp.int32)
    following = (lane + 1) & (LANES - 1)
    high_next = gather(high_bins, following)
    low_next = jnp.where(lane == LANES - 1, gather(high_bins, zero), gather(low_bins, following))

    def coded(bins, next_bins):
        value = gather(palette, bins) * FULL
        whole = (value + 0.5).astype(jnp.int32)
        change = (gather(palette, next_bins) * FULL - value) * 0.5 - whole.astype(jnp.float32) * (1.0 / 65536.0)
        step = (change + (HALF + 0.5)).astype(jnp.int32) - HALF
        return lax.shift_left(step, 16) | whole

    low_table = coded(low_bins, low_next)
    high_table = coded(high_bins, high_next)
    tables = []
    for channel in range(4):
        tables.append(
            tuple(jnp.broadcast_to(t[channel : channel + 1, :], (SUB, LANES)) for t in (low_table, high_table))
        )

    def send(turn):
        return pltpu.make_async_copy(staged.at[turn], out_ref.at[pl.ds(turn * STEP, STEP)], out_sems.at[turn])

    def some_tiles(turn, _):
        first = turn * STEP
        for part in range(CAP * STEP):
            fetch(first + part // CAP, part % CAP, 0).wait()
        for part in range(CAP * STEP):
            tile, rank = first + part // CAP, part % CAP
            filled = (found_scalar[tile] & (KEY << (SHIFT * rank))) != 0
            for field in range(4):
                cells32[part, field] = pages[tile, rank, field].astype(jnp.float32)
            for half in range(2):
                for odd in range(2):
                    colour = [None] * 3
                    through = None
                    before = None
                    for cell in range(4):
                        rows = pl.ds(64 * half + 4 * odd + cell, SUB, stride=8)
                        scalar, normal_x, normal_y, normal_z = (cells32[part, field, rows, :] for field in range(4))
                        scaled = scalar * (BINS - 1.0)
                        index = scaled.astype(jnp.int32)
                        up = (scaled - index.astype(jnp.float32)) * (1.0 / HALF)
                        upper_half = index >= LANES
                        lane_index = index & (LANES - 1)
                        rgba = []
                        for low, high in tables:
                            both = jnp.where(upper_half, gather(high, lane_index), gather(low, lane_index))
                            rgba.append((both & 0xFFFF).astype(jnp.float32) + both.astype(jnp.float32) * up)
                        facing = (
                            normal_x * (2 * LIGHT_X)
                            + normal_y * (2 * LIGHT_Y)
                            + normal_z * (2 * LIGHT_Z)
                            - (LIGHT_X + LIGHT_Y + LIGHT_Z)
                        )
                        shading = 1.0 + jnp.tanh(facing)
                        optical = rgba[3] * (-LOG2E / (16.0 * FULL))
                        through = optical if cell == 0 else through + optical
                        after = jnp.exp2(through)
                        weight = shading * ((1.0 if cell == 0 else before) - after)
                        before = after
                        for c in range(3):
                            term = rgba[c] * weight
                            colour[c] = term if cell == 0 else colour[c] + term
                    coded_parts = []
                    for c in range(3):
                        square = colour[c] * (0.5 * FULL / REACH)
                        root = square * lax.rsqrt(jnp.maximum(square, 1e-20))
                        coded_parts.append((root + 0.5).astype(jnp.int32))
                    coded_parts.append(((1.0 - before) * (FULL / REACH) + 0.5).astype(jnp.int32))
                    row = rank * 4 + odd
                    words = (
                        coded_parts[0] | lax.shift_left(coded_parts[1], 16),
                        coded_parts[2] | lax.shift_left(coded_parts[3], 16),
                    )
                    place = pl.ds(SUB * half, SUB)
                    for word in range(2):
                        staged[turn, part // CAP, place, row + 2 * word, :] = jnp.where(filled, words[word], 0)
        send(turn).start()
        return 0

    lax.fori_loop(0, tiles // STEP, some_tiles, 0)
    for turn in range(tiles // STEP):
        send(turn).wait()


def compose_kernel(source_ref, received_ref, out_ref, ordered, *, depths, per_tile):
    groups = per_tile // SUB

    def one_depth(depth, state):
        for foot in range(per_tile):
            source = pl.multiple_of(source_ref[depth, foot], 4)
            ordered[depth, 4 * foot : 4 * foot + 4, :] = received_ref[pl.ds(source, 4), :]
        new = []
        for group in range(groups):
            for odd in range(2):
                red, green, blue, clear = state[group * 2 + odd]
                first = ordered[depth, pl.ds(32 * group + odd, SUB, stride=4), :]
                second = ordered[depth, pl.ds(32 * group + 2 + odd, SUB, stride=4), :]

                def squared(x):
                    x = x.astype(jnp.float32)
                    return x * x

                scaled = clear * (REACH / (FULL * FULL))
                red = red + scaled * squared(first & 0xFFFF)
                green = green + scaled * squared(lax.shift_right_logical(first, 16))
                blue = blue + scaled * squared(second & 0xFFFF)
                clear = clear - clear * (lax.shift_right_logical(second, 16).astype(jnp.float32) * (REACH / FULL))
                new.append((red, green, blue, clear))
        return new

    none = jnp.zeros((SUB, LANES), jnp.float32)
    state = [(none, none, none, none + 1.0) for _ in range(groups * 2)]
    state = lax.fori_loop(0, depths, one_depth, state, unroll=16)
    for group in range(groups):
        for odd in range(2):
            for c in range(4):
                out_ref[c, SUB * group : SUB * group + SUB, LANES * odd : LANES * odd + LANES] = state[group * 2 + odd][c]


def render_messages(page_table, tf_bins, palette, pool):
    page_count, cells, pixels = pool.shape[1], pool.shape[3], pool.shape[4]
    depths, tiles = pixels // SHARE, page_table.shape[1] // FOOT
    columns = pixels // LANES
    bricks = pool[0].reshape(page_count, 4, cells, columns, LANES).transpose(0, 1, 3, 2, 4)
    bricks = bricks.reshape(page_count, 4, columns * cells, LANES)
    return pl.pallas_call(
        functools.partial(render_kernel, tiles=tiles, page_count=page_count),
        out_shape=jax.ShapeDtypeStruct((tiles, depths, SUB, LANES), jnp.int32),
        in_specs=[
            pl.BlockSpec(memory_space=pltpu.VMEM),
            pl.BlockSpec(memory_space=pltpu.VMEM),
            pl.BlockSpec(memory_space=pltpu.VMEM),
            pl.BlockSpec(memory_space=pltpu.HBM),
        ],
        out_specs=pl.BlockSpec(memory_space=pltpu.HBM),
        scratch_shapes=[
            pltpu.VMEM((tiles, CAP, 4, columns * cells, LANES), jnp.bfloat16),
            pltpu.VMEM((CAP * STEP, 4, columns * cells, LANES), jnp.float32),
            pltpu.VMEM((SUB, LANES), jnp.float32),
            pltpu.VMEM((tiles // STEP, STEP, depths, SUB, LANES), jnp.int32),
            pltpu.SMEM((tiles,), jnp.int32),
            pltpu.SemaphoreType.DMA((tiles, CAP)),
            pltpu.SemaphoreType.DMA((tiles // STEP,)),
        ],
        compiler_params=pltpu.CompilerParams(vmem_limit_bytes=60 * 1024 * 1024),
        name="render",
    )(page_table.reshape(FOOT * tiles // LANES, LANES), tf_bins.reshape(2, LANES), palette, bricks)


def per_device(pool, page_table, tf_bins, palette):
    tiles = lax.axis_size("tile")
    depths = lax.axis_size("depth")
    tile = lax.axis_index("tile")
    page_count, cells, pixels = pool.shape[1], pool.shape[3], pool.shape[4]
    per_tile = page_table.shape[1] // tiles

    rows = page_table[:, :]
    gathered = lax.all_gather(rows, "depth", axis=0, tiled=True)

    messages = render_messages(page_table, tf_bins, palette, pool)
    received = lax.all_to_all(
        messages.reshape(tiles * depths, SUB, LANES), ("tile", "depth"), split_axis=0, concat_axis=0, tiled=True
    )

    own = lax.dynamic_slice_in_dim(gathered, tile * per_tile, per_tile, 1)
    holder = jnp.where(own >= 0, own // page_count, -1)
    foot = jnp.arange(per_tile)
    earlier = (holder[:, :, None] == holder[:, None, :]) & (foot[None, :, None] > foot[None, None, :])
    rank = jnp.any(earlier, axis=2).astype(jnp.int32)
    source = (holder * depths + jnp.arange(depths)[:, None]) * CAP + rank
    held = jnp.sum((holder[:, None, :] == jnp.arange(tiles)[None, :, None]).astype(jnp.int32), axis=2)
    last = (jnp.arange(tiles)[None, :] * depths + jnp.arange(depths)[:, None]) * CAP + CAP - 1
    empty = jnp.max(jnp.where(held < CAP, last, 0), axis=1)
    source = jnp.where(own >= 0, source, empty[:, None]) * 4

    return pl.pallas_call(
        functools.partial(compose_kernel, depths=depths, per_tile=per_tile),
        out_shape=jax.ShapeDtypeStruct((4, per_tile, pixels // depths), jnp.float32),
        in_specs=[pl.BlockSpec(memory_space=pltpu.SMEM), pl.BlockSpec(memory_space=pltpu.VMEM)],
        out_specs=pl.BlockSpec(memory_space=pltpu.VMEM),
        scratch_shapes=[pltpu.VMEM((depths, 4 * per_tile, LANES), jnp.int32)],
        compiler_params=pltpu.CompilerParams(vmem_limit_bytes=24 * 1024 * 1024),
        name="compose",
    )(source, received.reshape(depths * tiles * SUB, LANES))


def solution(mesh):
    in_specs = (P("depth", "tile", None, None, None), P("depth", None), P(), P())
    out_specs = P(None, "tile", "depth")
    return jax.shard_map(per_device, mesh=mesh, in_specs=in_specs, out_specs=out_specs, check_vma=False)
```

```python
import functools
import math

import jax
import jax.numpy as jnp
from jax import lax
from jax.experimental import pallas as pl
from jax.experimental.pallas import tpu as pltpu
from jax.sharding import PartitionSpec as P

BINS = 256
LANES = 128
SUB = 8
CAP = 2
FOOT = 32
SHARE = 256
LIGHT_X = 0.48
LIGHT_Y = 0.6
LIGHT_Z = 0.64
LOG2E = 1.4426950408889634
FULL = 65535.0
HALF = 32768
REACH = 0.2213
SCALE = 0.5 * FULL / REACH
SCALE_LOG2 = math.log2(SCALE)
KEY = 64
SHIFT = 16
STEP = 4


def render_kernel(
    table_ref, bins_ref, palette_ref, pool_ref, out_ref, pages, cells32, wide, staged, found_scalar, sems, out_sems, *, tiles, page_count
):
    local = table_ref[...] - lax.axis_index("tile") * page_count
    here = (local >= 0) & (local < page_count)
    key = (lax.broadcasted_iota(jnp.int32, local.shape, 1) & (FOOT - 1)) * KEY + local
    ends = jnp.concatenate([jnp.where(here, key, FOOT * KEY), jnp.where(here, -key, 1)], axis=0)
    step = 1
    while step < FOOT:
        ends = jnp.minimum(ends, pltpu.roll(ends, step, 1))
        step *= 2
    least, largest = ends[: local.shape[0]], -ends[local.shape[0] :]
    one = jnp.where(largest >= 0, KEY | (least & (KEY - 1)), 0)
    two = jnp.where(largest > least, KEY | (largest & (KEY - 1)), 0)
    both_found = one | lax.shift_left(two, SHIFT)
    picked = [both_found[tile // 4, (tile % 4) * FOOT + FOOT - 1] for tile in range(tiles)]

    def fetch(tile, rank, page):
        return pltpu.make_async_copy(pool_ref.at[page], pages.at[tile, rank], sems.at[tile, rank])

    def begin(tile):
        both = picked[tile]
        found_scalar[tile] = both
        fetch(tile, 0, both & (KEY - 1)).start()
        fetch(tile, 1, lax.shift_right_logical(both, SHIFT) & (KEY - 1)).start()

    for tile in range(tiles):
        begin(tile)

    def gather(table, index):
        return jnp.take_along_axis(table, index, axis=1, mode="promise_in_bounds")

    wide[...] = jnp.zeros_like(wide)
    wide[0:4, 0:16] = palette_ref[...]
    palette = wide[...]
    low_bins = jnp.broadcast_to(bins_ref[0:1, :], (SUB, LANES))
    high_bins = jnp.broadcast_to(bins_ref[1:2, :], (SUB, LANES))
    lane = lax.broadcasted_iota(jnp.int32, (SUB, LANES), 1)

    def colours(bin_index):
        at = bin_index & (LANES - 1)
        bins = jnp.where(bin_index < LANES, gather(low_bins, at), gather(high_bins, at))
        return gather(palette, bins) * FULL

    first, middle, after_it = colours(2 * lane), colours(2 * lane + 1), colours(jnp.minimum(2 * lane + 2, BINS - 1))

    def step_code(change, low_bits):
        return (change * 0.5 - low_bits.astype(jnp.float32) * (1.0 / 65536.0) + (HALF + 0.5)).astype(jnp.int32) - HALF

    whole = (middle + 0.5).astype(jnp.int32)
    to_table = lax.shift_left(step_code(middle - first, whole), 16) | whole
    change = after_it - middle
    lower = step_code(change, jnp.zeros_like(whole)) & 0xFFFF
    to_tables = [jnp.broadcast_to(to_table[c : c + 1, :], (SUB, LANES)) for c in range(4)]
    from_tables = []
    for c in range(0, 4, 2):
        low_row = jnp.broadcast_to(lower[c + 1 : c + 2, :], (SUB, LANES))
        row = jnp.broadcast_to(change[c : c + 1, :], (SUB, LANES))
        from_tables.append(lax.shift_left(step_code(row, low_row), 16) | low_row)

    def send(turn):
        return pltpu.make_async_copy(staged.at[turn], out_ref.at[pl.ds(turn * STEP, STEP)], out_sems.at[turn])

    def some_tiles(turn, _):
        first = turn * STEP
        for part in range(CAP * STEP):
            fetch(first + part // CAP, part % CAP, 0).wait()
        for part in range(CAP * STEP):
            tile, rank = first + part // CAP, part % CAP
            filled = (found_scalar[tile] & (KEY << (SHIFT * rank))) != 0
            scalar, normal_x, normal_y, normal_z = (pages[tile, rank, field].astype(jnp.float32) for field in range(4))
            facing = (
                normal_x * (2 * LIGHT_X)
                + normal_y * (2 * LIGHT_Y)
                + normal_z * (2 * LIGHT_Z)
                - (LIGHT_X + LIGHT_Y + LIGHT_Z)
            )
            cells32[part, 0] = scalar * ((BINS - 1.0) / 2)
            cells32[part, 1] = 1.0 + jnp.tanh(facing)
            for half in range(2):
                for odd in range(2):
                    colour = [None] * 3
                    through = None
                    before = None
                    for cell in range(4):
                        rows = pl.ds(64 * half + 4 * odd + cell, SUB, stride=8)
                        scaled = cells32[part, 0, rows, :]
                        index = scaled.astype(jnp.int32)
                        along = (scaled - index.astype(jnp.float32) - 0.5) * (2.0 / HALF)
                        to_it, from_it = jnp.minimum(along, 0.0), jnp.maximum(along, 0.0)
                        lane_index = index & (LANES - 1)
                        tos = [gather(table, lane_index) for table in to_tables]
                        froms = []
                        for table in from_tables:
                            both = gather(table, lane_index)
                            froms += [both, lax.shift_left(both, 16)]
                        rgba = []
                        for word, step_on in zip(tos, froms):
                            value = (word & 0xFFFF).astype(jnp.float32) + word.astype(jnp.float32) * to_it
                            rgba.append(value + step_on.astype(jnp.float32) * from_it)
                        shading = cells32[part, 1, rows, :]
                        optical = rgba[3] * (-LOG2E / (16.0 * FULL))
                        through = optical + SCALE_LOG2 if cell == 0 else through + optical
                        after = jnp.exp2(through)
                        weight = shading * ((SCALE if cell == 0 else before) - after)
                        before = after
                        for c in range(3):
                            term = rgba[c] * weight
                            colour[c] = term if cell == 0 else colour[c] + term
                    coded_parts = []
                    for c in range(3):
                        square = colour[c]
                        root = square * lax.rsqrt(jnp.maximum(square, 1e-20))
                        coded_parts.append((root + 0.5).astype(jnp.int32))
                    coded_parts.append(((2 * SCALE + 0.5) - before * 2.0).astype(jnp.int32))
                    row = rank * 4 + odd
                    words = (
                        coded_parts[0] | lax.shift_left(coded_parts[1], 16),
                        coded_parts[2] | lax.shift_left(coded_parts[3], 16),
                    )
                    place = pl.ds(SUB * half, SUB)
                    for word in range(2):
                        staged[turn, part // CAP, place, row + 2 * word, :] = jnp.where(filled, words[word], 0)
        send(turn).start()
        return 0

    lax.fori_loop(0, tiles // STEP, some_tiles, 0)
    for turn in range(tiles // STEP):
        send(turn).wait()


def compose_kernel(source_ref, received_ref, out_ref, ordered, *, depths, per_tile):
    groups = per_tile // SUB

    def one_depth(depth, state):
        for foot in range(per_tile):
            source = pl.multiple_of(source_ref[depth, foot], 4)
            ordered[depth, 4 * foot : 4 * foot + 4, :] = received_ref[pl.ds(source, 4), :]
        new = []
        for group in range(groups):
            for odd in range(2):
                red, green, blue, clear = state[group * 2 + odd]
                first = ordered[depth, pl.ds(32 * group + odd, SUB, stride=4), :]
                second = ordered[depth, pl.ds(32 * group + 2 + odd, SUB, stride=4), :]

                def squared(x):
                    x = x.astype(jnp.float32)
                    return x * x

                scaled = clear * (REACH / (FULL * FULL))
                red = red + scaled * squared(first & 0xFFFF)
                green = green + scaled * squared(lax.shift_right_logical(first, 16))
                blue = blue + scaled * squared(second & 0xFFFF)
                clear = clear - clear * (lax.shift_right_logical(second, 16).astype(jnp.float32) * (REACH / FULL))
                new.append((red, green, blue, clear))
        return new

    none = jnp.zeros((SUB, LANES), jnp.float32)
    state = [(none, none, none, none + 1.0) for _ in range(groups * 2)]
    state = lax.fori_loop(0, depths, one_depth, state, unroll=16)
    for group in range(groups):
        for odd in range(2):
            for c in range(4):
                out_ref[c, SUB * group : SUB * group + SUB, LANES * odd : LANES * odd + LANES] = state[group * 2 + odd][c]


def render_messages(page_table, tf_bins, palette, pool):
    page_count, cells, pixels = pool.shape[1], pool.shape[3], pool.shape[4]
    depths, tiles = pixels // SHARE, page_table.shape[1] // FOOT
    columns = pixels // LANES
    bricks = pool[0].reshape(page_count, 4, cells, columns, LANES).transpose(0, 1, 3, 2, 4)
    bricks = bricks.reshape(page_count, 4, columns * cells, LANES)
    return pl.pallas_call(
        functools.partial(render_kernel, tiles=tiles, page_count=page_count),
        out_shape=jax.ShapeDtypeStruct((tiles, depths, SUB, LANES), jnp.int32),
        in_specs=[
            pl.BlockSpec(memory_space=pltpu.VMEM),
            pl.BlockSpec(memory_space=pltpu.VMEM),
            pl.BlockSpec(memory_space=pltpu.VMEM),
            pl.BlockSpec(memory_space=pltpu.HBM),
        ],
        out_specs=pl.BlockSpec(memory_space=pltpu.HBM),
        scratch_shapes=[
            pltpu.VMEM((tiles, CAP, 4, columns * cells, LANES), jnp.bfloat16),
            pltpu.VMEM((CAP * STEP, 2, columns * cells, LANES), jnp.float32),
            pltpu.VMEM((SUB, LANES), jnp.float32),
            pltpu.VMEM((tiles // STEP, STEP, depths, SUB, LANES), jnp.int32),
            pltpu.SMEM((tiles,), jnp.int32),
            pltpu.SemaphoreType.DMA((tiles, CAP)),
            pltpu.SemaphoreType.DMA((tiles // STEP,)),
        ],
        compiler_params=pltpu.CompilerParams(vmem_limit_bytes=60 * 1024 * 1024),
        name="render",
    )(page_table.reshape(FOOT * tiles // LANES, LANES), tf_bins.reshape(2, LANES), palette, bricks)


def per_device(pool, page_table, tf_bins, palette):
    tiles = lax.axis_size("tile")
    depths = lax.axis_size("depth")
    tile = lax.axis_index("tile")
    page_count, cells, pixels = pool.shape[1], pool.shape[3], pool.shape[4]
    per_tile = page_table.shape[1] // tiles

    rows = page_table[:, :]
    gathered = lax.all_gather(rows, "depth", axis=0, tiled=True)

    messages = render_messages(page_table, tf_bins, palette, pool)
    received = lax.all_to_all(
        messages.reshape(tiles * depths, SUB, LANES), ("tile", "depth"), split_axis=0, concat_axis=0, tiled=True
    )

    own = lax.dynamic_slice_in_dim(gathered, tile * per_tile, per_tile, 1)
    holder = jnp.where(own >= 0, own // page_count, -1)
    foot = jnp.arange(per_tile)
    earlier = (holder[:, :, None] == holder[:, None, :]) & (foot[None, :, None] > foot[None, None, :])
    rank = jnp.any(earlier, axis=2).astype(jnp.int32)
    source = (holder * depths + jnp.arange(depths)[:, None]) * CAP + rank
    held = jnp.sum((holder[:, None, :] == jnp.arange(tiles)[None, :, None]).astype(jnp.int32), axis=2)
    last = (jnp.arange(tiles)[None, :] * depths + jnp.arange(depths)[:, None]) * CAP + CAP - 1
    empty = jnp.max(jnp.where(held < CAP, last, 0), axis=1)
    source = jnp.where(own >= 0, source, empty[:, None]) * 4

    return pl.pallas_call(
        functools.partial(compose_kernel, depths=depths, per_tile=per_tile),
        out_shape=jax.ShapeDtypeStruct((4, per_tile, pixels // depths), jnp.float32),
        in_specs=[pl.BlockSpec(memory_space=pltpu.SMEM), pl.BlockSpec(memory_space=pltpu.VMEM)],
        out_specs=pl.BlockSpec(memory_space=pltpu.VMEM),
        scratch_shapes=[pltpu.VMEM((depths, 4 * per_tile, LANES), jnp.int32)],
        compiler_params=pltpu.CompilerParams(vmem_limit_bytes=24 * 1024 * 1024),
        name="compose",
    )(source, received.reshape(depths * tiles * SUB, LANES))


def solution(mesh):
    in_specs = (P("depth", "tile", None, None, None), P("depth", None), P(), P())
    out_specs = P(None, "tile", "depth")
    return jax.shard_map(per_device, mesh=mesh, in_specs=in_specs, out_specs=out_specs, check_vma=False)
```

```python
import functools

import jax
import jax.numpy as jnp
from jax import lax
from jax.experimental import pallas as pl
from jax.experimental.pallas import tpu as pltpu
from jax.sharding import PartitionSpec as P

BINS = 256
LANES = 128
SUB = 8
CAP = 2
FOOT = 32
SHARE = 256
LIGHT_X = 0.48
LIGHT_Y = 0.6
LIGHT_Z = 0.64
LOG2E = 1.4426950408889634
FULL = 65535.0
HALF = 32768
REACH = 0.2213
KEY = 64
SHIFT = 16
STEP = 4


def render_kernel(
    table_ref, bins_ref, palette_ref, pool_ref, out_ref, pages, cells32, wide, staged, found_scalar, sems, out_sems, *, tiles, page_count
):
    local = table_ref[...] - lax.axis_index("tile") * page_count
    here = (local >= 0) & (local < page_count)
    key = (lax.broadcasted_iota(jnp.int32, local.shape, 1) & (FOOT - 1)) * KEY + local
    least = jnp.where(here, key, FOOT * KEY)
    largest = jnp.where(here, key, -1)
    step = 1
    while step < FOOT:
        least = jnp.minimum(least, pltpu.roll(least, step, 1))
        largest = jnp.maximum(largest, pltpu.roll(largest, step, 1))
        step *= 2
    one = jnp.where(largest >= 0, KEY | (least & (KEY - 1)), 0)
    two = jnp.where(largest > least, KEY | (largest & (KEY - 1)), 0)
    both_found = one | lax.shift_left(two, SHIFT)
    picked = [both_found[tile // 4, (tile % 4) * FOOT + FOOT - 1] for tile in range(tiles)]

    def fetch(tile, rank, page):
        return pltpu.make_async_copy(pool_ref.at[page], pages.at[tile, rank], sems.at[tile, rank])

    def begin(tile):
        both = picked[tile]
        found_scalar[tile] = both
        fetch(tile, 0, both & (KEY - 1)).start()
        fetch(tile, 1, lax.shift_right_logical(both, SHIFT) & (KEY - 1)).start()

    for tile in range(tiles):
        begin(tile)

    def gather(table, index):
        return jnp.take_along_axis(table, index, axis=1, mode="promise_in_bounds")

    wide[...] = jnp.zeros_like(wide)
    wide[0:4, 0:16] = palette_ref[...]
    palette = wide[...]
    low_bins = jnp.broadcast_to(bins_ref[0:1, :], (SUB, LANES))
    high_bins = jnp.broadcast_to(bins_ref[1:2, :], (SUB, LANES))
    lane = lax.broadcasted_iota(jnp.int32, (SUB, LANES), 1)
    zero = jnp.zeros((SUB, LANES), jnp.int32)
    following = (lane + 1) & (LANES - 1)
    high_next = gather(high_bins, following)
    low_next = jnp.where(lane == LANES - 1, gather(high_bins, zero), gather(low_bins, following))

    def coded(bins, next_bins):
        value = gather(palette, bins) * FULL
        whole = (value + 0.5).astype(jnp.int32)
        change = (gather(palette, next_bins) * FULL - value) * 0.5 - whole.astype(jnp.float32) * (1.0 / 65536.0)
        step = (change + (HALF + 0.5)).astype(jnp.int32) - HALF
        return lax.shift_left(step, 16) | whole

    low_table = coded(low_bins, low_next)
    high_table = coded(high_bins, high_next)
    tables = []
    for channel in range(4):
        tables.append(
            tuple(jnp.broadcast_to(t[channel : channel + 1, :], (SUB, LANES)) for t in (low_table, high_table))
        )

    def send(turn):
        return pltpu.make_async_copy(staged.at[turn], out_ref.at[pl.ds(turn * STEP, STEP)], out_sems.at[turn])

    def some_tiles(turn, _):
        first = turn * STEP
        for part in range(CAP * STEP):
            fetch(first + part // CAP, part % CAP, 0).wait()
        for part in range(CAP * STEP):
            tile, rank = first + part // CAP, part % CAP
            filled = (found_scalar[tile] & (KEY << (SHIFT * rank))) != 0
            for field in range(4):
                cells32[part, field] = pages[tile, rank, field].astype(jnp.float32)
            for half in range(2):
                for odd in range(2):
                    colour = [None] * 3
                    through = None
                    before = None
                    for cell in range(4):
                        rows = pl.ds(64 * half + 4 * odd + cell, SUB, stride=8)
                        scalar, normal_x, normal_y, normal_z = (cells32[part, field, rows, :] for field in range(4))
                        scaled = scalar * (BINS - 1.0)
                        index = scaled.astype(jnp.int32)
                        up = (scaled - index.astype(jnp.float32)) * (1.0 / HALF)
                        upper_half = index >= LANES
                        lane_index = index & (LANES - 1)
                        rgba = []
                        for low, high in tables:
                            both = jnp.where(upper_half, gather(high, lane_index), gather(low, lane_index))
                            rgba.append((both & 0xFFFF).astype(jnp.float32) + both.astype(jnp.float32) * up)
                        facing = (
                            normal_x * (2 * LIGHT_X)
                            + normal_y * (2 * LIGHT_Y)
                            + normal_z * (2 * LIGHT_Z)
                            - (LIGHT_X + LIGHT_Y + LIGHT_Z)
                        )
                        shading = 1.0 + jnp.tanh(facing)
                        optical = rgba[3] * (-LOG2E / (16.0 * FULL))
                        through = optical if cell == 0 else through + optical
                        after = jnp.exp2(through)
                        weight = shading * ((1.0 if cell == 0 else before) - after)
                        before = after
                        for c in range(3):
                            term = rgba[c] * weight
                            colour[c] = term if cell == 0 else colour[c] + term
                    coded_parts = []
                    for c in range(3):
                        square = colour[c] * (0.5 * FULL / REACH)
                        root = square * lax.rsqrt(jnp.maximum(square, 1e-20))
                        coded_parts.append((root + 0.5).astype(jnp.int32))
                    coded_parts.append(((1.0 - before) * (FULL / REACH) + 0.5).astype(jnp.int32))
                    row = rank * 4 + odd
                    words = (
                        coded_parts[0] | lax.shift_left(coded_parts[1], 16),
                        coded_parts[2] | lax.shift_left(coded_parts[3], 16),
                    )
                    place = pl.ds(SUB * half, SUB)
                    for word in range(2):
                        staged[turn, part // CAP, place, row + 2 * word, :] = jnp.where(filled, words[word], 0)
        send(turn).start()
        return 0

    lax.fori_loop(0, tiles // STEP, some_tiles, 0)
    for turn in range(tiles // STEP):
        send(turn).wait()


def compose_kernel(source_ref, received_ref, out_ref, ordered, *, depths, per_tile):
    groups = per_tile // SUB

    def one_depth(depth, state):
        for foot in range(per_tile):
            source = pl.multiple_of(source_ref[depth, foot], 4)
            ordered[depth, 4 * foot : 4 * foot + 4, :] = received_ref[pl.ds(source, 4), :]
        new = []
        for group in range(groups):
            for odd in range(2):
                red, green, blue, clear = state[group * 2 + odd]
                first = ordered[depth, pl.ds(32 * group + odd, SUB, stride=4), :]
                second = ordered[depth, pl.ds(32 * group + 2 + odd, SUB, stride=4), :]

                def squared(x):
                    x = x.astype(jnp.float32)
                    return x * x

                scaled = clear * (REACH / (FULL * FULL))
                red = red + scaled * squared(first & 0xFFFF)
                green = green + scaled * squared(lax.shift_right_logical(first, 16))
                blue = blue + scaled * squared(second & 0xFFFF)
                clear = clear - clear * (lax.shift_right_logical(second, 16).astype(jnp.float32) * (REACH / FULL))
                new.append((red, green, blue, clear))
        return new

    none = jnp.zeros((SUB, LANES), jnp.float32)
    state = [(none, none, none, none + 1.0) for _ in range(groups * 2)]
    state = lax.fori_loop(0, depths, one_depth, state, unroll=16)
    for group in range(groups):
        for odd in range(2):
            for c in range(4):
                out_ref[c, SUB * group : SUB * group + SUB, LANES * odd : LANES * odd + LANES] = state[group * 2 + odd][c]


def render_messages(page_table, tf_bins, palette, pool):
    page_count, cells, pixels = pool.shape[1], pool.shape[3], pool.shape[4]
    depths, tiles = pixels // SHARE, page_table.shape[1] // FOOT
    columns = pixels // LANES
    bricks = pool[0].reshape(page_count, 4, cells, columns, LANES).transpose(0, 1, 3, 2, 4)
    bricks = bricks.reshape(page_count, 4, columns * cells, LANES)
    return pl.pallas_call(
        functools.partial(render_kernel, tiles=tiles, page_count=page_count),
        out_shape=jax.ShapeDtypeStruct((tiles, depths, SUB, LANES), jnp.int32),
        in_specs=[
            pl.BlockSpec(memory_space=pltpu.VMEM),
            pl.BlockSpec(memory_space=pltpu.VMEM),
            pl.BlockSpec(memory_space=pltpu.VMEM),
            pl.BlockSpec(memory_space=pltpu.HBM),
        ],
        out_specs=pl.BlockSpec(memory_space=pltpu.HBM),
        scratch_shapes=[
            pltpu.VMEM((tiles, CAP, 4, columns * cells, LANES), jnp.bfloat16),
            pltpu.VMEM((CAP * STEP, 4, columns * cells, LANES), jnp.float32),
            pltpu.VMEM((SUB, LANES), jnp.float32),
            pltpu.VMEM((tiles // STEP, STEP, depths, SUB, LANES), jnp.int32),
            pltpu.SMEM((tiles,), jnp.int32),
            pltpu.SemaphoreType.DMA((tiles, CAP)),
            pltpu.SemaphoreType.DMA((tiles // STEP,)),
        ],
        compiler_params=pltpu.CompilerParams(vmem_limit_bytes=60 * 1024 * 1024),
        name="render",
    )(page_table.reshape(FOOT * tiles // LANES, LANES), tf_bins.reshape(2, LANES), palette, bricks)


def per_device(pool, page_table, tf_bins, palette):
    tiles = lax.axis_size("tile")
    depths = lax.axis_size("depth")
    tile = lax.axis_index("tile")
    page_count, cells, pixels = pool.shape[1], pool.shape[3], pool.shape[4]
    per_tile = page_table.shape[1] // tiles

    own_row = lax.dynamic_slice_in_dim(page_table, tile * per_tile, per_tile, 1)
    own = lax.all_gather(own_row, "depth", axis=0, tiled=True)

    messages = render_messages(page_table, tf_bins, palette, pool)
    received = lax.all_to_all(
        messages.reshape(tiles * depths, SUB, LANES), ("tile", "depth"), split_axis=0, concat_axis=0, tiled=True
    )

    holder = jnp.where(own >= 0, own // page_count, -1)
    foot = jnp.arange(per_tile)
    earlier = (holder[:, :, None] == holder[:, None, :]) & (foot[None, :, None] > foot[None, None, :])
    rank = jnp.any(earlier, axis=2).astype(jnp.int32)
    source = (holder * depths + jnp.arange(depths)[:, None]) * CAP + rank
    held = jnp.sum((holder[:, None, :] == jnp.arange(tiles)[None, :, None]).astype(jnp.int32), axis=2)
    last = (jnp.arange(tiles)[None, :] * depths + jnp.arange(depths)[:, None]) * CAP + CAP - 1
    empty = jnp.max(jnp.where(held < CAP, last, 0), axis=1)
    source = jnp.where(own >= 0, source, empty[:, None]) * 4

    return pl.pallas_call(
        functools.partial(compose_kernel, depths=depths, per_tile=per_tile),
        out_shape=jax.ShapeDtypeStruct((4, per_tile, pixels // depths), jnp.float32),
        in_specs=[pl.BlockSpec(memory_space=pltpu.SMEM), pl.BlockSpec(memory_space=pltpu.VMEM)],
        out_specs=pl.BlockSpec(memory_space=pltpu.VMEM),
        scratch_shapes=[pltpu.VMEM((depths, 4 * per_tile, LANES), jnp.int32)],
        compiler_params=pltpu.CompilerParams(vmem_limit_bytes=24 * 1024 * 1024),
        name="compose",
    )(source, received.reshape(depths * tiles * SUB, LANES))


def solution(mesh):
    in_specs = (P("depth", "tile", None, None, None), P("depth", None), P(), P())
    out_specs = P(None, "tile", "depth")
    return jax.shard_map(per_device, mesh=mesh, in_specs=in_specs, out_specs=out_specs, check_vma=False)
```

```python
import functools
import math

import jax
import jax.numpy as jnp
from jax import lax
from jax.experimental import pallas as pl
from jax.experimental.pallas import tpu as pltpu
from jax.sharding import PartitionSpec as P

BINS = 256
LANES = 128
SUB = 8
CAP = 2
FOOT = 32
SHARE = 256
LIGHT_X = 0.48
LIGHT_Y = 0.6
LIGHT_Z = 0.64
LOG2E = 1.4426950408889634
FULL = 65535.0
HALF = 32768
REACH = 0.2213
SCALE = 0.5 * FULL / REACH
SCALE_LOG2 = math.log2(SCALE)
KEY = 64
SHIFT = 16
STEP = 4


def render_kernel(
    table_ref, bins_ref, palette_ref, pool_ref, out_ref, pages, cells32, wide, staged, found_scalar, sems, out_sems, *, tiles, page_count
):
    local = table_ref[...] - lax.axis_index("tile") * page_count
    here = (local >= 0) & (local < page_count)
    key = (lax.broadcasted_iota(jnp.int32, local.shape, 1) & (FOOT - 1)) * KEY + local
    ends = jnp.concatenate([jnp.where(here, key, FOOT * KEY), jnp.where(here, -key, 1)], axis=0)
    step = 1
    while step < FOOT:
        ends = jnp.minimum(ends, pltpu.roll(ends, step, 1))
        step *= 2
    least, largest = ends[: local.shape[0]], -ends[local.shape[0] :]
    one = jnp.where(largest >= 0, KEY | (least & (KEY - 1)), 0)
    two = jnp.where(largest > least, KEY | (largest & (KEY - 1)), 0)
    both_found = one | lax.shift_left(two, SHIFT)
    picked = [both_found[tile // 4, (tile % 4) * FOOT + FOOT - 1] for tile in range(tiles)]

    def fetch(tile, rank, page):
        return pltpu.make_async_copy(pool_ref.at[page], pages.at[tile, rank], sems.at[tile, rank])

    def begin(tile):
        both = picked[tile]
        found_scalar[tile] = both
        fetch(tile, 0, both & (KEY - 1)).start()
        fetch(tile, 1, lax.shift_right_logical(both, SHIFT) & (KEY - 1)).start()

    for tile in range(tiles):
        begin(tile)

    def gather(table, index):
        return jnp.take_along_axis(table, index, axis=1, mode="promise_in_bounds")

    wide[...] = jnp.zeros_like(wide)
    wide[0:4, 0:16] = palette_ref[...]
    palette = wide[...]
    low_bins = jnp.broadcast_to(bins_ref[0:1, :], (SUB, LANES))
    high_bins = jnp.broadcast_to(bins_ref[1:2, :], (SUB, LANES))
    lane = lax.broadcasted_iota(jnp.int32, (SUB, LANES), 1)

    def colours(bin_index):
        at = bin_index & (LANES - 1)
        bins = jnp.where(bin_index < LANES, gather(low_bins, at), gather(high_bins, at))
        return gather(palette, bins) * FULL

    first, middle, after_it = colours(2 * lane), colours(2 * lane + 1), colours(jnp.minimum(2 * lane + 2, BINS - 1))

    def step_code(change, low_bits):
        return (change * 0.5 - low_bits.astype(jnp.float32) * (1.0 / 65536.0) + (HALF + 0.5)).astype(jnp.int32) - HALF

    whole = (middle + 0.5).astype(jnp.int32)
    to_table = lax.shift_left(step_code(middle - first, whole), 16) | whole
    change = after_it - middle
    lower = step_code(change, jnp.zeros_like(whole)) & 0xFFFF
    to_tables = [jnp.broadcast_to(to_table[c : c + 1, :], (SUB, LANES)) for c in range(4)]
    from_tables = []
    for c in range(0, 4, 2):
        low_row = jnp.broadcast_to(lower[c + 1 : c + 2, :], (SUB, LANES))
        row = jnp.broadcast_to(change[c : c + 1, :], (SUB, LANES))
        from_tables.append(lax.shift_left(step_code(row, low_row), 16) | low_row)

    def send(turn):
        return pltpu.make_async_copy(staged.at[turn], out_ref.at[pl.ds(turn * STEP, STEP)], out_sems.at[turn])

    def some_tiles(turn, _):
        first = turn * STEP
        for part in range(CAP * STEP):
            fetch(first + part // CAP, part % CAP, 0).wait()
        for part in range(CAP * STEP):
            tile, rank = first + part // CAP, part % CAP
            filled = (found_scalar[tile] & (KEY << (SHIFT * rank))) != 0
            scalar, normal_x, normal_y, normal_z = (pages[tile, rank, field].astype(jnp.float32) for field in range(4))
            facing = (
                normal_x * (2 * LIGHT_X)
                + normal_y * (2 * LIGHT_Y)
                + normal_z * (2 * LIGHT_Z)
                - (LIGHT_X + LIGHT_Y + LIGHT_Z)
            )
            cells32[part, 0] = scalar * ((BINS - 1.0) / 2)
            cells32[part, 1] = 1.0 + jnp.tanh(facing)
            for half in range(2):
                for odd in range(2):
                    colour = [None] * 3
                    through = None
                    before = None
                    for cell in range(4):
                        rows = pl.ds(64 * half + 4 * odd + cell, SUB, stride=8)
                        scaled = cells32[part, 0, rows, :]
                        index = scaled.astype(jnp.int32)
                        along = (scaled - index.astype(jnp.float32) - 0.5) * (2.0 / HALF)
                        to_it, from_it = jnp.minimum(along, 0.0), jnp.maximum(along, 0.0)
                        lane_index = index & (LANES - 1)
                        tos = [gather(table, lane_index) for table in to_tables]
                        froms = []
                        for table in from_tables:
                            both = gather(table, lane_index)
                            froms += [both, lax.shift_left(both, 16)]
                        rgba = []
                        for word, step_on in zip(tos, froms):
                            value = (word & 0xFFFF).astype(jnp.float32) + word.astype(jnp.float32) * to_it
                            rgba.append(value + step_on.astype(jnp.float32) * from_it)
                        shading = cells32[part, 1, rows, :]
                        optical = rgba[3] * (-LOG2E / (16.0 * FULL))
                        through = optical + SCALE_LOG2 if cell == 0 else through + optical
                        after = jnp.exp2(through)
                        weight = shading * ((SCALE if cell == 0 else before) - after)
                        before = after
                        for c in range(3):
                            term = rgba[c] * weight
                            colour[c] = term if cell == 0 else colour[c] + term
                    coded_parts = []
                    for c in range(3):
                        square = colour[c]
                        root = square * lax.rsqrt(jnp.maximum(square, 1e-20))
                        coded_parts.append((root + 0.5).astype(jnp.int32))
                    coded_parts.append(((2 * SCALE + 0.5) - before * 2.0).astype(jnp.int32))
                    row = rank * 4 + odd
                    words = (
                        coded_parts[0] | lax.shift_left(coded_parts[1], 16),
                        coded_parts[2] | lax.shift_left(coded_parts[3], 16),
                    )
                    place = pl.ds(SUB * half, SUB)
                    for word in range(2):
                        staged[turn, part // CAP, place, row + 2 * word, :] = jnp.where(filled, words[word], 0)
        send(turn).start()
        return 0

    lax.fori_loop(0, tiles // STEP, some_tiles, 0)
    for turn in range(tiles // STEP):
        send(turn).wait()


def compose_kernel(source_ref, received_ref, out_ref, ordered, *, depths, per_tile):
    groups = per_tile // SUB

    def one_depth(depth, state):
        for foot in range(per_tile):
            source = pl.multiple_of(source_ref[depth, foot], 4)
            ordered[depth, 4 * foot : 4 * foot + 4, :] = received_ref[pl.ds(source, 4), :]
        new = []
        for group in range(groups):
            for odd in range(2):
                red, green, blue, clear = state[group * 2 + odd]
                first = ordered[depth, pl.ds(32 * group + odd, SUB, stride=4), :]
                second = ordered[depth, pl.ds(32 * group + 2 + odd, SUB, stride=4), :]

                def squared(x):
                    x = x.astype(jnp.float32)
                    return x * x

                scaled = clear * (REACH / (FULL * FULL))
                red = red + scaled * squared(first & 0xFFFF)
                green = green + scaled * squared(lax.shift_right_logical(first, 16))
                blue = blue + scaled * squared(second & 0xFFFF)
                clear = clear - clear * (lax.shift_right_logical(second, 16).astype(jnp.float32) * (REACH / FULL))
                new.append((red, green, blue, clear))
        return new

    none = jnp.zeros((SUB, LANES), jnp.float32)
    state = [(none, none, none, none + 1.0) for _ in range(groups * 2)]
    state = lax.fori_loop(0, depths, one_depth, state, unroll=16)
    for group in range(groups):
        for odd in range(2):
            for c in range(4):
                out_ref[c, SUB * group : SUB * group + SUB, LANES * odd : LANES * odd + LANES] = state[group * 2 + odd][c]


def render_messages(page_table, tf_bins, palette, pool):
    page_count, cells, pixels = pool.shape[1], pool.shape[3], pool.shape[4]
    depths, tiles = pixels // SHARE, page_table.shape[1] // FOOT
    columns = pixels // LANES
    bricks = pool[0].reshape(page_count, 4, cells, columns, LANES).transpose(0, 1, 3, 2, 4)
    bricks = bricks.reshape(page_count, 4, columns * cells, LANES)
    return pl.pallas_call(
        functools.partial(render_kernel, tiles=tiles, page_count=page_count),
        out_shape=jax.ShapeDtypeStruct((tiles, depths, SUB, LANES), jnp.int32),
        in_specs=[
            pl.BlockSpec(memory_space=pltpu.VMEM),
            pl.BlockSpec(memory_space=pltpu.VMEM),
            pl.BlockSpec(memory_space=pltpu.VMEM),
            pl.BlockSpec(memory_space=pltpu.HBM),
        ],
        out_specs=pl.BlockSpec(memory_space=pltpu.HBM),
        scratch_shapes=[
            pltpu.VMEM((tiles, CAP, 4, columns * cells, LANES), jnp.bfloat16),
            pltpu.VMEM((CAP * STEP, 2, columns * cells, LANES), jnp.float32),
            pltpu.VMEM((SUB, LANES), jnp.float32),
            pltpu.VMEM((tiles // STEP, STEP, depths, SUB, LANES), jnp.int32),
            pltpu.SMEM((tiles,), jnp.int32),
            pltpu.SemaphoreType.DMA((tiles, CAP)),
            pltpu.SemaphoreType.DMA((tiles // STEP,)),
        ],
        compiler_params=pltpu.CompilerParams(vmem_limit_bytes=60 * 1024 * 1024),
        name="render",
    )(page_table.reshape(FOOT * tiles // LANES, LANES), tf_bins.reshape(2, LANES), palette, bricks)


def per_device(pool, page_table, tf_bins, palette):
    tiles = lax.axis_size("tile")
    depths = lax.axis_size("depth")
    tile = lax.axis_index("tile")
    page_count, cells, pixels = pool.shape[1], pool.shape[3], pool.shape[4]
    per_tile = page_table.shape[1] // tiles

    own_row = lax.dynamic_slice_in_dim(page_table, tile * per_tile, per_tile, 1)
    own = lax.all_gather(own_row, "depth", axis=0, tiled=True)

    messages = render_messages(page_table, tf_bins, palette, pool)
    received = lax.all_to_all(
        messages.reshape(tiles * depths, SUB, LANES), ("tile", "depth"), split_axis=0, concat_axis=0, tiled=True
    )

    holder = jnp.where(own >= 0, own // page_count, -1)
    foot = jnp.arange(per_tile)
    earlier = (holder[:, :, None] == holder[:, None, :]) & (foot[None, :, None] > foot[None, None, :])
    rank = jnp.any(earlier, axis=2).astype(jnp.int32)
    source = (holder * depths + jnp.arange(depths)[:, None]) * CAP + rank
    held = jnp.sum((holder[:, None, :] == jnp.arange(tiles)[None, :, None]).astype(jnp.int32), axis=2)
    last = (jnp.arange(tiles)[None, :] * depths + jnp.arange(depths)[:, None]) * CAP + CAP - 1
    empty = jnp.max(jnp.where(held < CAP, last, 0), axis=1)
    source = jnp.where(own >= 0, source, empty[:, None]) * 4

    return pl.pallas_call(
        functools.partial(compose_kernel, depths=depths, per_tile=per_tile),
        out_shape=jax.ShapeDtypeStruct((4, per_tile, pixels // depths), jnp.float32),
        in_specs=[pl.BlockSpec(memory_space=pltpu.SMEM), pl.BlockSpec(memory_space=pltpu.VMEM)],
        out_specs=pl.BlockSpec(memory_space=pltpu.VMEM),
        scratch_shapes=[pltpu.VMEM((depths, 4 * per_tile, LANES), jnp.int32)],
        compiler_params=pltpu.CompilerParams(vmem_limit_bytes=24 * 1024 * 1024),
        name="compose",
    )(source, received.reshape(depths * tiles * SUB, LANES))


def solution(mesh):
    in_specs = (P("depth", "tile", None, None, None), P("depth", None), P(), P())
    out_specs = P(None, "tile", "depth")
    return jax.shard_map(per_device, mesh=mesh, in_specs=in_specs, out_specs=out_specs, check_vma=False)
```
